32 devices in a mesh: row: 4 (over y, core), col: 8 (over z, x).
Axes of the slice: x: 2, y: 2, z: 4, core: 2. Of those that a mesh axis runs over, the one named last changes fastest.
Arguments:
- object_amp: float32 [4, 2048, 4096], P(None, 'row', 'col'), may hold values from 0.5 to 1.5
- object_phase: float32 [4, 2048, 4096], P(None, 'row', 'col'), may hold values from -3.140625 to 3.140625
- probe_field: float32 [2, 256, 256], replicated, may hold values from -5 to 5
- measured: float32 [4, 8, 4, 256, 256], P('row', 'col'), may hold values from 0 to 2
- offsets: int32 [4, 8, 4, 2], P('row', 'col'), may hold values from 0 to 512
- counts: int32 [4, 8], P('row', 'col'), may hold values from 1 to 4, as said below
Outputs:
- new_real: float32 [4, 2048, 4096], P(None, 'row', 'col')
- new_imag: float32 [4, 2048, 4096], P(None, 'row', 'col')
The draws below stay inside these ranges and needn't reach their ends.
Inputs may be any that keep to these rules, and one draw needn't show every extreme that they name: `counts`: every count is at least one, and some tile uses all 4 slots. Slots at or beyond a tile's count are unused. `offsets`: entries of unused slots carry no meaning.
All inputs are finite; a program needn't handle non-finite values.
Results may differ from the reference program's by a relative error of at most 0.0003.
Values sent between devices are 32-bit elements; how exact they have to be, the bound alone decides.
A program may use at most 192 MiB of HBM per device.

```python
import jax
import jax.numpy as jnp
from jax import lax

P_SIZE = 256
SL = 4
MAXPOS = 4
TILE = 512
TROWS = 4
TCOLS = 8
ROWS = 2048
COLS = 4096


def draw_counts(key, part):
    first_key, second_key, third_key = jax.random.split(jax.random.fold_in(key, 17), 3)
    first = jax.random.randint(first_key, (TROWS, TCOLS), 0, 3)
    second = jax.random.randint(second_key, (TROWS, TCOLS), 0, 3)
    base = jnp.minimum(1 + first + second, MAXPOS)
    chosen = jax.random.randint(third_key, (), 0, TROWS * TCOLS)
    flat_counts = base.reshape(-1)
    flat_counts = jnp.where(jnp.arange(TROWS * TCOLS) == chosen, MAXPOS, flat_counts)
    return flat_counts.reshape(TROWS, TCOLS).astype(jnp.int32)


def touch_ends(entries, own_key, low, top_value):
    shape = entries.shape
    place = [jax.random.randint(jax.random.fold_in(own_key, axis), (), 0, shape[axis]) for axis in range(len(shape))]
    entries = entries.at[tuple(place)].set(low)
    longest = shape.index(max(shape))
    place[longest] = (place[longest] + 1) % shape[longest]
    return entries.at[tuple(place)].set(top_value)


def level_of(rng, extent, cuts, low, top_value):
    factor_of = 1.0
    for axis_at, blocks in cuts:
        steps = jax.random.uniform(jax.random.fold_in(jax.random.fold_in(rng, 6), axis_at), (blocks,), jnp.float32, low / len(cuts), top_value / len(cuts))
        factor_of = factor_of * jnp.repeat(jnp.exp(steps), extent[axis_at] // blocks).reshape((-1,) + (1,) * (len(extent) - 1 - axis_at))
    return factor_of


def bell_draw(rng, shape, scale, limit, kind=jnp.bfloat16):
    drawn = jax.random.normal(rng, shape, jnp.float32) * scale
    return jnp.minimum(jnp.maximum(drawn, -limit), limit).astype(kind)


def setup_inputs(seed: int = 0) -> dict:
    key_list = jax.random.split(jax.random.key(seed), 7)
    return {
        "object_amp": jnp.clip(1.0 + 0.1 * jax.random.normal(key_list[0], (SL, ROWS, COLS), jnp.float32), 0.5, 1.5),
        "object_phase": jnp.clip(jax.random.uniform(key_list[1], (SL, ROWS, COLS), jnp.float32, -3.140625, 3.140625), -3.140625, 3.140625),
        "probe_field": bell_draw(key_list[2], (2, P_SIZE, P_SIZE), 0.7, 5.0, jnp.float32),
        "measured": jnp.clip(2.0 * jax.random.uniform(key_list[3], (TROWS, TCOLS, MAXPOS, P_SIZE, P_SIZE), jnp.float32) ** level_of(key_list[3], (TROWS, TCOLS, MAXPOS, P_SIZE, P_SIZE), ((0, 4), (1, 8)), -0.2, 0.2), 0.0, 2.0),
        "offsets": touch_ends(jax.random.randint(key_list[4], (TROWS, TCOLS, MAXPOS, 2), 0, TILE + 1), jax.random.fold_in(key_list[4], 1), 0, TILE).astype(jnp.int32),
        "counts": draw_counts(jax.random.fold_in(key_list[6], 71), 0),
    }


FRESNEL = 0.0005


def forward_fft(field):
    return jnp.fft.fft2(field, norm="ortho")


def inverse_fft(field):
    return jnp.fft.ifft2(field, norm="ortho")


def position_terms(window, target, probe_wave, kernel):
    wave = probe_wave
    incident = []
    exit_wave = wave
    for layer in range(SL):
        incident.append(wave)
        exit_wave = wave * window[layer]
        if layer + 1 < SL:
            wave = inverse_fft(forward_fft(exit_wave) * kernel)
    far = forward_fft(exit_wave)
    misfit = far.real * far.real + far.imag * far.imag - target
    back = inverse_fft(misfit * far)
    grads = [None] * SL
    lights = [None] * SL
    for layer in reversed(range(SL)):
        here = incident[layer]
        grads[layer] = jnp.conj(here) * back
        lights[layer] = here.real * here.real + here.imag * here.imag
        if layer > 0:
            back = inverse_fft(forward_fft(jnp.conj(window[layer]) * back) * jnp.conj(kernel))
    return jnp.stack(grads), jnp.stack(lights)


def reference(object_amp, object_phase, probe_field, measured, offsets, counts):
    width = P_SIZE // 2
    slab = lax.complex(object_amp * jnp.cos(object_phase), object_amp * jnp.sin(object_phase))
    padded = jnp.pad(slab, ((0, 0), (width, width), (width, width)))
    probe_wave = lax.complex(probe_field[0], probe_field[1])
    counter = jnp.arange(P_SIZE, dtype=jnp.int32)
    frequency = (((counter + P_SIZE // 2) % P_SIZE) - P_SIZE // 2).astype(jnp.float32)
    phases = FRESNEL * (frequency[:, None] ** 2 + frequency[None, :] ** 2)
    kernel = lax.complex(jnp.cos(phases), jnp.sin(phases))
    slot_total = TROWS * TCOLS * MAXPOS
    order_ids = jnp.arange(slot_total, dtype=jnp.int32)
    tile_row = order_ids // (TCOLS * MAXPOS)
    tile_col = (order_ids // MAXPOS) % TCOLS
    slot_ids = order_ids % MAXPOS
    live = (slot_ids < counts[tile_row, tile_col]).astype(jnp.float32)
    tops = (tile_row * TILE + offsets[tile_row, tile_col, slot_ids, 0]).astype(jnp.int32)
    lefts = (tile_col * TILE + offsets[tile_row, tile_col, slot_ids, 1]).astype(jnp.int32)
    flat_measured = measured.reshape(slot_total, P_SIZE, P_SIZE)
    grad_start = jnp.zeros(padded.shape, dtype=padded.dtype)
    light_start = jnp.zeros(padded.shape, dtype=object_amp.dtype)

    def visit(carry, item):
        grad_total, light_total = carry
        top, left, weight, target = item
        start = (jnp.int32(0), top.astype(jnp.int32), left.astype(jnp.int32))
        window = lax.dynamic_slice(padded, start, (SL, P_SIZE, P_SIZE))
        grads, lights = position_terms(window, target, probe_wave, kernel)
        grad_total = lax.dynamic_update_slice(grad_total, lax.dynamic_slice(grad_total, start, (SL, P_SIZE, P_SIZE)) + weight * grads, start)
        light_total = lax.dynamic_update_slice(light_total, lax.dynamic_slice(light_total, start, (SL, P_SIZE, P_SIZE)) + weight * lights, start)
        return (grad_total, light_total), None

    (grad_total, light_total), _ = lax.scan(visit, (grad_start, light_start), (tops, lefts, live, flat_measured))
    grad_total = grad_total[:, width:width + ROWS, width:width + COLS]
    light_total = light_total[:, width:width + ROWS, width:width + COLS]
    updated = slab - grad_total / (light_total + 1.0)
    return updated.real, updated.imag
```

```python
import functools
import math

import jax
import jax.numpy as jnp
import numpy as np
import ml_dtypes
from jax import lax
from jax.experimental import pallas as pl
from jax.experimental.pallas import tpu as pltpu
from jax.sharding import PartitionSpec as P

FRESNEL = 0.0005
LANES = 128
SUBLANES = 8
VMEM_BYTES = 50 * 1024 * 1024


def shifted(value, axis, steps):
    count = lax.axis_size(axis)
    first, last = (max(0, -steps), min(count, count - steps))
    return lax.ppermute(value, axis, [(source, source + steps) for source in range(first, last)])


def sine_cosine(angle):
    half = angle * 0.5
    square = half * half
    sine = 1.0 / 6227020800.0
    for order in (11, 9, 7, 5, 3, 1):
        sign = -1.0 if (order // 2) % 2 else 1.0
        sine = sine * square + sign / math.factorial(order)
    sine = sine * half
    cosine = -1.0 / math.factorial(14)
    for order in (12, 10, 8, 6, 4, 2, 0):
        sign = -1.0 if (order // 2) % 2 else 1.0
        cosine = cosine * square + sign / math.factorial(order)
    return 2.0 * sine * cosine, 1.0 - 2.0 * sine * sine


def halves(table):
    high = table.astype(ml_dtypes.bfloat16)
    low = (table - high.astype(np.float64)).astype(ml_dtypes.bfloat16)
    return high, low


def make_tables(extent):
    half = extent // 2
    inner = np.arange(half)
    lefts, rights = [], []
    for parity in (0, 1):
        turn = np.outer(2 * inner + parity, inner) % extent
        wave = np.exp(-2j * np.pi * turn / extent) / math.sqrt(extent)
        block = np.block([[wave.real, -wave.imag], [wave.imag, wave.real]])
        for table in (block, block.T):
            high, low = halves(table)
            lefts.append(np.concatenate([high, high, low], 1))
            rights.append(np.concatenate([high, high, low], 0))
    order = np.concatenate([np.arange(0, extent, 2), np.arange(1, extent, 2)])
    frequency = ((order + half) % extent - half).astype(np.float64)
    phases = FRESNEL * (frequency[:, None] ** 2 + frequency[None, :] ** 2)
    fresnel = np.stack([np.cos(phases), np.sin(phases)]).astype(np.float32)
    pick = np.zeros((extent, extent), np.float32)
    pick[order, np.arange(extent)] = 1.0
    pick = np.stack([pick, pick.T]).astype(ml_dtypes.bfloat16)
    return np.stack(lefts), np.stack(rights), fresnel, pick


def split(value):
    high = value.astype(jnp.bfloat16)
    return high, (value - high.astype(jnp.float32)).astype(jnp.bfloat16)


def dot_left(table, value):
    high, low = split(value)
    return jnp.dot(table, jnp.concatenate([high, low, high], 0), preferred_element_type=jnp.float32)


def dot_right(value, table):
    high, low = split(value)
    return jnp.dot(jnp.concatenate([high, low, high], 1), table, preferred_element_type=jnp.float32)


def pieces(value):
    high, rest = split(value)
    low = (value - high.astype(jnp.float32)) - rest.astype(jnp.float32)
    return high, rest, low.astype(jnp.bfloat16)


def permuted(value, pick):
    value = sum(jnp.dot(piece, pick[0], preferred_element_type=jnp.float32) for piece in pieces(value))
    return sum(jnp.dot(pick[1], piece, preferred_element_type=jnp.float32) for piece in pieces(value))


def forward(wave, left, right):
    real, imag = wave
    h = real.shape[0] // 2
    even = dot_left(left[0], jnp.concatenate([real[:h] + real[h:], imag[:h] + imag[h:]], 0))
    odd = dot_left(left[2], jnp.concatenate([real[:h] - real[h:], imag[:h] - imag[h:]], 0))
    real = jnp.concatenate([even[:h], odd[:h]], 0)
    imag = jnp.concatenate([even[h:], odd[h:]], 0)
    even = dot_right(jnp.concatenate([real[:, :h] + real[:, h:], imag[:, :h] + imag[:, h:]], 1), right[1])
    odd = dot_right(jnp.concatenate([real[:, :h] - real[:, h:], imag[:, :h] - imag[:, h:]], 1), right[3])
    return (jnp.concatenate([even[:, :h], odd[:, :h]], 1), jnp.concatenate([even[:, h:], odd[:, h:]], 1))


def inverse(wave, left, right):
    real, imag = wave
    h = real.shape[0] // 2
    even = dot_right(jnp.concatenate([real[:, :h], imag[:, :h]], 1), right[0])
    odd = dot_right(jnp.concatenate([real[:, h:], imag[:, h:]], 1), right[2])
    total, other = even + odd, even - odd
    real = jnp.concatenate([total[:, :h], other[:, :h]], 1)
    imag = jnp.concatenate([total[:, h:], other[:, h:]], 1)
    even = dot_left(left[1], jnp.concatenate([real[:h], imag[:h]], 0))
    odd = dot_left(left[3], jnp.concatenate([real[h:], imag[h:]], 0))
    total, other = even + odd, even - odd
    return (jnp.concatenate([total[:h], other[:h]], 0), jnp.concatenate([total[h:], other[h:]], 0))


def product_of(first, second):
    return (
        first[0] * second[0] - first[1] * second[1],
        first[0] * second[1] + first[1] * second[0],
    )


def conj_product(first, second):
    return (
        first[0] * second[0] + first[1] * second[1],
        first[0] * second[1] - first[1] * second[0],
    )


def place(offset_ref, slot, side, extent):
    spot = []
    for axis, unit in ((0, SUBLANES), (1, LANES)):
        start = offset_ref[slot, axis]
        base = jnp.minimum(start // unit * unit, side - extent - unit)
        spot += [pl.multiple_of(base, unit), start - base]
    return spot


def window_of(padded_ref, plane, spot, extent):
    top, down, base, shift = spot
    wide = padded_ref[plane, pl.ds(top, extent + SUBLANES), pl.ds(base, extent + LANES)]
    wide = pltpu.roll(wide, extent + LANES - shift, 1)[:, :extent]
    return pltpu.roll(wide, extent + SUBLANES - down, 0)[:extent]


def add_window(total_ref, plane, spot, piece):
    top, down, base, shift = spot
    extent = piece.shape[0]
    wide = jnp.concatenate([piece, jnp.zeros((SUBLANES, extent), jnp.float32)], 0)
    wide = pltpu.roll(wide, down, 0)
    wide = jnp.concatenate([wide, jnp.zeros((extent + SUBLANES, LANES), jnp.float32)], 1)
    total_ref[plane, pl.ds(top, extent + SUBLANES), pl.ds(base, extent + LANES)] += pltpu.roll(wide, shift, 1)


def light_of(wave):
    return wave[0] * wave[0] + wave[1] * wave[1]


def clear_first(slot, total_ref):
    @pl.when(slot == 0)
    def _():
        total_ref[...] = jnp.zeros_like(total_ref)


def forward_kernel(offset_ref, count_ref, padded_ref, wave_ref, left, right, fresnel, next_ref, window_ref, light_ref):
    slot = pl.program_id(0)
    clear_first(slot, light_ref)

    @pl.when(slot < count_ref[0])
    def _():
        extent = wave_ref.shape[-1]
        spot = place(offset_ref, slot, padded_ref.shape[-1], extent)
        wave = (wave_ref[0, 0], wave_ref[0, 1])
        window = (window_of(padded_ref, 0, spot, extent), window_of(padded_ref, 1, spot, extent))
        window_ref[0, 0] = window[0]
        window_ref[0, 1] = window[1]
        add_window(light_ref, 0, spot, light_of(wave))
        spectrum = forward(product_of(wave, window), left, right)
        after = inverse(product_of(spectrum, (fresnel[0], fresnel[1])), left, right)
        next_ref[0, 0] = after[0]
        next_ref[0, 1] = after[1]


def middle_kernel(offset_ref, count_ref, padded_ref, wave_ref, measured_ref, left, right, fresnel, pick, back_ref, total_ref):
    slot = pl.program_id(0)
    clear_first(slot, total_ref)

    @pl.when(slot < count_ref[0])
    def _():
        extent = wave_ref.shape[-1]
        h = extent // 2
        spot = place(offset_ref, slot, padded_ref.shape[-1], extent)
        wave = (wave_ref[0, 0], wave_ref[0, 1])
        window = (window_of(padded_ref, 0, spot, extent), window_of(padded_ref, 1, spot, extent))
        add_window(total_ref, 2, spot, light_of(wave))
        far = forward(product_of(wave, window), left, right)
        target = permuted(measured_ref[0], pick)
        misfit = light_of(far) - target
        back = inverse((misfit * far[0], misfit * far[1]), left, right)
        grad = conj_product(wave, back)
        add_window(total_ref, 0, spot, grad[0])
        add_window(total_ref, 1, spot, grad[1])
        spectrum = forward(conj_product(window, back), left, right)
        back = inverse(conj_product((fresnel[0], fresnel[1]), spectrum), left, right)
        back_ref[0, 0] = back[0]
        back_ref[0, 1] = back[1]


def backward_kernel(offset_ref, count_ref, wave_ref, window_ref, back_in, left, right, fresnel, back_ref, total_ref):
    slot = pl.program_id(0)
    clear_first(slot, total_ref)

    @pl.when(slot < count_ref[0])
    def _():
        extent = wave_ref.shape[-1]
        spot = place(offset_ref, slot, total_ref.shape[-1], extent)
        wave = (wave_ref[0, 0], wave_ref[0, 1])
        back = (back_in[0, 0], back_in[0, 1])
        grad = conj_product(wave, back)
        add_window(total_ref, 0, spot, grad[0])
        add_window(total_ref, 1, spot, grad[1])
        if back_ref is not None:
            spectrum = forward(conj_product((window_ref[0, 0], window_ref[0, 1]), back), left, right)
            back = inverse(conj_product((fresnel[0], fresnel[1]), spectrum), left, right)
            back_ref[0, 0] = back[0]
            back_ref[0, 1] = back[1]


def last_kernel(offset_ref, count_ref, wave_ref, back_in, total_ref):
    backward_kernel(offset_ref, count_ref, wave_ref, None, back_in, None, None, None, None, total_ref)


def body(object_amp, object_phase, probe_field, measured, offsets, counts):
    layers, tile_side = object_amp.shape[0], object_amp.shape[1]
    extent = probe_field.shape[1]
    slots = measured.shape[2]
    width = extent // 2
    side = tile_side + 2 * width
    left, right, fresnel, pick = (jnp.asarray(table) for table in make_tables(extent))

    def whole(array):
        return pl.BlockSpec(array.shape, lambda s, *_: (0,) * array.ndim)

    def per_slot(array):
        if array.shape[0] == 1:
            return whole(array)
        return pl.BlockSpec((1,) + array.shape[1:], lambda s, *_: (s,) + (0,) * (array.ndim - 1))

    waves = jax.ShapeDtypeStruct((slots, 2, extent, extent), jnp.float32)

    def planes(count):
        return jax.ShapeDtypeStruct((count, side, side), jnp.float32)

    def call(kernel, ins, outs, transforms):
        flops = transforms * slots * 2 * 4 * 3 * extent**3
        moved = sum(4 * math.prod(x.shape) for x in [a for a, _ in ins] + [a for a, _ in outs])
        return pl.pallas_call(
            kernel,
            grid_spec=pltpu.PrefetchScalarGridSpec(
                num_scalar_prefetch=2,
                grid=(slots,),
                in_specs=[spec(array) for array, spec in ins],
                out_specs=[spec(array) for array, spec in outs],
            ),
            out_shape=[array for array, _ in outs],
            compiler_params=pltpu.CompilerParams(vmem_limit_bytes=VMEM_BYTES, dimension_semantics=("arbitrary",)),
            cost_estimate=pl.CostEstimate(flops=flops, bytes_accessed=moved, transcendentals=0),
        )(offsets[0, 0], counts[0], *[array for array, _ in ins])

    tables = [(left, whole), (right, whole), (fresnel, whole)]

    sine, cosine = sine_cosine(object_phase)
    slab_real, slab_imag = object_amp * cosine, object_amp * sine

    def halo(layer):
        tile = jnp.stack([slab_real[layer], slab_imag[layer]])
        before = shifted(tile[:, :, -width:], "col", 1)
        after = shifted(tile[:, :, :width], "col", -1)
        tile = jnp.concatenate([before, tile, after], 2)
        above = shifted(tile[:, -width:], "row", 1)
        below = shifted(tile[:, :width], "row", -1)
        return jnp.concatenate([above, tile, below], 1)

    def fold(totals):
        from_next = shifted(totals[:, :width], "row", -1)
        from_prev = shifted(totals[:, -width:], "row", 1)
        rest = tile_side - width
        centre = totals[:, width:-width]
        centre = centre + jnp.pad(from_prev, ((0, 0), (0, rest), (0, 0))) + jnp.pad(from_next, ((0, 0), (rest, 0), (0, 0)))
        from_next = shifted(centre[:, :, :width], "col", -1)
        from_prev = shifted(centre[:, :, -width:], "col", 1)
        centre = centre[:, :, width:-width]
        return centre + jnp.pad(from_prev, ((0, 0), (0, 0), (0, rest))) + jnp.pad(from_next, ((0, 0), (0, 0), (rest, 0)))

    padded = [halo(layer) for layer in range(layers)]
    wave = probe_field[None]
    incident, windows, lights = [], [], []
    for layer in range(layers - 1):
        incident.append(wave)
        wave, window, light = call(
            forward_kernel,
            [(padded[layer], whole), (wave, per_slot)] + tables,
            [(waves, per_slot), (waves, per_slot), (planes(1), whole)],
            2,
        )
        windows.append(window)
        lights.append(fold(light)[0])
    back, total = call(
        middle_kernel,
        [(padded[-1], whole), (wave, per_slot), (measured[0, 0], per_slot)] + tables + [(pick, whole)],
        [(waves, per_slot), (planes(3), whole)],
        4,
    )
    total = fold(total)
    lights.append(total[2])
    grads = [total[:2]]
    for layer in reversed(range(layers - 1)):
        if layer > 0:
            back, total = call(
                backward_kernel,
                [(incident[layer], per_slot), (windows[layer], per_slot), (back, per_slot)] + tables,
                [(waves, per_slot), (planes(2), whole)],
                2,
            )
        else:
            (total,) = call(last_kernel, [(incident[0], per_slot), (back, per_slot)], [(planes(2), whole)], 0)
        grads.insert(0, fold(total))
    new_real = [slab_real[s] - grads[s][0] / (lights[s] + 1.0) for s in range(layers)]
    new_imag = [slab_imag[s] - grads[s][1] / (lights[s] + 1.0) for s in range(layers)]
    return (jnp.stack(new_real), jnp.stack(new_imag))


def solution(mesh):
    placed = (
        P(None, "row", "col"),
        P(None, "row", "col"),
        P(),
        P("row", "col", None, None, None),
        P("row", "col", None, None),
        P("row", "col"),
    )
    return jax.shard_map(
        body,
        mesh=mesh,
        in_specs=placed,
        out_specs=(P(None, "row", "col"), P(None, "row", "col")),
        check_vma=False,
    )
```
